1024 devices in a mesh: row: 64 (over y, z_hi, x), col: 16 (over z_lo, core).
Axes of the slice: x: 4, y: 4, z: 32 (z_hi: 4, z_lo: 8; z = z_hi * 8 + z_lo), core: 2. Of those that a mesh axis runs over, the one named last changes fastest.
Arguments:
- vectors: bfloat16 [8, 1048576], P(None, ('row', 'col')), may hold values from -6 to 6
- tile_blocks: bfloat16 [64, 16, 16, 256, 256], P('row', 'col'), may hold values from -0.375 to 0.375
- block_pairs: int32 [64, 16, 16, 2], P('row', 'col'), may hold values from 0 to 63
- tile_counts: int32 [64, 16], P('row', 'col'), may hold values from 2 to 16, as said below
Outputs:
- product: float32 [8, 1048576], P(None, ('row', 'col'))
The draws below stay inside these ranges and needn't reach their ends.
Inputs may be any that keep to these rules, and one draw needn't show every extreme that they name: `tile_counts`: some tile (r, c) with r + c < 64 has exactly 16 live slots.
All inputs are finite; a program needn't handle non-finite values.
Results may differ from the reference program's by a relative error of at most 0.0003.
Values may be sent and summed in bfloat16 or wider, within the bound.
No kernel may reach another device: no remote copies, remote signals or barrier semaphores. Data moves between devices by JAX's collectives and lax.ppermute only.
A program may use at most 64 MiB of HBM per device.

```python
import jax
import jax.numpy as jnp
from jax import lax

VECS = 8
SEG = 16384
BLK = 256
KMAX = 16
NTOT = 1048576
N_ROW = 64
N_COL = 16


def draw_tile_counts(key, part):
    key = jax.random.fold_in(key, 5)
    key_base, key_heavy, key_row, key_diag = jax.random.split(key, 4)
    base_counts = jax.random.randint(key_base, (N_ROW, N_COL), KMAX // 8, KMAX // 2 + 1)
    heavy_tiles = jax.random.randint(key_heavy, (N_ROW, N_COL), 0, 8) == 0
    forced_row = jax.random.randint(key_row, (), 0, N_ROW - N_COL + 1)
    forced_diag = jax.random.randint(key_diag, (), 0, N_COL)
    row_range = jnp.arange(N_ROW, dtype=jnp.int32)[:, None]
    diag_range = jnp.arange(N_COL, dtype=jnp.int32)[None, :]
    forced_tile = (row_range == forced_row) & (diag_range == forced_diag)
    return jnp.where(heavy_tiles | forced_tile, KMAX, base_counts).astype(jnp.int32)


def touch_ends(result, key, low, top_value):
    shape = result.shape
    spot = [jax.random.randint(jax.random.fold_in(key, axis), (), 0, shape[axis]) for axis in range(len(shape))]
    result = result.at[tuple(spot)].set(low)
    longest = shape.index(max(shape))
    spot[longest] = (spot[longest] + 1) % shape[longest]
    return result.at[tuple(spot)].set(top_value)


def steps_of(stream_key, shape, shards, least, largest):
    factor_of = 1.0
    for position, parts in shards:
        steps = jax.random.uniform(jax.random.fold_in(jax.random.fold_in(stream_key, 6), position), (parts,), jnp.float32, least / len(shards), largest / len(shards))
        factor_of = factor_of * jnp.repeat(jnp.exp(steps), shape[position] // parts).reshape((-1,) + (1,) * (len(shape) - 1 - position))
    return factor_of


def noise(rng, shape, deviation, bound, shards=(), held_as=jnp.bfloat16):
    values = jax.random.normal(rng, shape, jnp.float32) * deviation
    if len(shards) > 0:
        values = steps_of(rng, shape, shards, -0.22, 0.18) * values
    return jnp.clip(values, min=-bound, max=bound).astype(held_as)


def setup_inputs(seed: int = 0) -> dict:
    seeds = jax.random.split(jax.random.key(seed), 5)
    vectors = noise(seeds[0], (VECS, NTOT), 1.0, 6.0, ((1, 1024),))
    tile_blocks = noise(seeds[1], (N_ROW, N_COL, KMAX, BLK, BLK), BLK ** -0.5, 0.375, ((0, 64), (1, 16)))
    block_pairs = touch_ends(jax.random.randint(seeds[2], (N_ROW, N_COL, KMAX, 2), 0, SEG // BLK), jax.random.fold_in(seeds[2], 1), 0, (SEG // BLK) - 1).astype(jnp.int32)
    tile_counts = draw_tile_counts(jax.random.fold_in(seeds[4], 71), 0)
    return {"vectors": vectors, "tile_blocks": tile_blocks, "block_pairs": block_pairs, "tile_counts": tile_counts}


def reference(vectors, tile_blocks, block_pairs, tile_counts):
    vec_count = vectors.shape[0]
    block_count = SEG // BLK
    shaped = vectors.astype(jnp.float32).reshape(vec_count, N_ROW, block_count, BLK)

    def one_tile(tile_number, running):
        row_number = tile_number // N_COL
        diag_number = tile_number % N_COL
        blocks = tile_blocks[row_number, diag_number].astype(jnp.float32)
        pair_rows = block_pairs[row_number, diag_number]
        upper_row = jnp.minimum(row_number + diag_number, N_ROW - 1)
        live_slots = (jnp.arange(KMAX) < tile_counts[row_number, diag_number]) & (row_number + diag_number < N_ROW)
        weight = jnp.where(live_slots, 1.0, 0.0).astype(jnp.float32)
        near_rows = shaped[:, row_number][:, pair_rows[:, 1]]
        far_rows = shaped[:, upper_row][:, pair_rows[:, 0]]
        normal = jnp.einsum("vka,kba->vkb", near_rows, blocks, precision=lax.Precision.HIGHEST) * weight[None, :, None]
        transposed = jnp.einsum("vkb,kba->vka", far_rows, blocks, precision=lax.Precision.HIGHEST) * weight[None, :, None]
        running = running.at[:, upper_row, pair_rows[:, 0]].add(normal)
        running = running.at[:, row_number, pair_rows[:, 1]].add(transposed)
        return running

    initial = jnp.zeros((vec_count, N_ROW, block_count, BLK), jnp.float32)
    summed = lax.fori_loop(0, N_ROW * N_COL, one_tile, initial)
    return summed.reshape(vec_count, N_ROW * SEG)
```

```python
import functools

import jax
import jax.numpy as jnp
from jax import lax
from jax.experimental import pallas as pl
from jax.experimental.pallas import tpu as pltpu
from jax.sharding import PartitionSpec as P


def place_of(block, own, digits, per_piece):
    mixed = (block // per_piece) ^ own
    turned = jnp.int32(0)
    for bit in range(digits):
        turned = turned | (((mixed >> bit) & 1) << (digits - 1 - bit))
    return turned * per_piece + block % per_piece


def pick_kernel(near_index, far_index, own_ref, segment, near_rows, far_rows, *, digits, per_piece):
    slots, _, width = near_rows.shape
    own = own_ref[0]
    for index, rows in ((far_index, far_rows), (near_index, near_rows)):
        for slot in range(slots):
            place = place_of(index[slot], own, digits, per_piece)
            rows[slot] = segment[:, pl.ds(pl.multiple_of(place * width, width), width)]


def add_kernel(near_index, far_index, own_ref, count_ref, trans, arrived, total, *, digits, per_piece):
    slots, _, width = trans.shape
    own = own_ref[0]
    count = count_ref[0]
    total[...] = jnp.zeros_like(total)
    for slot in range(slots):
        place = place_of(near_index[slot], own, digits, per_piece)
        where = pl.ds(pl.multiple_of(place * width, width), width)
        total[:, where] += jnp.where(slot < count, trans[slot], 0.0)
        place = place_of(far_index[slot], own, digits, per_piece)
        where = pl.ds(pl.multiple_of(place * width, width), width)
        total[:, where] += arrived[slot]


def body(vectors, tile_blocks, block_pairs, tile_counts):
    row_count = lax.axis_size("row")
    col_count = lax.axis_size("col")
    col_index = lax.axis_index("col")
    row_index = lax.axis_index("row")
    digits = col_count.bit_length() - 1
    blocks = tile_blocks[0, 0]
    pair_rows = block_pairs[0, 0, :, 0]
    pair_cols = block_pairs[0, 0, :, 1]
    slots, width, _ = blocks.shape
    vec_count, piece = vectors.shape
    per_piece = piece // width
    own = col_index.astype(jnp.int32)[None]
    in_band = row_index + col_index < row_count
    count = jnp.where(in_band, tile_counts[0, 0], 0)
    up = [(r * col_count + c, (r + c) * col_count + c)
          for r in range(row_count) for c in range(col_count) if r + c < row_count]
    down = [(b, a) for a, b in up]
    both = ("row", "col")

    far_index = lax.ppermute(pair_rows, both, up)
    segment = vectors
    for bit in reversed(range(digits)):
        pairs = [(c, c ^ (1 << bit)) for c in range(col_count)]
        segment = jnp.concatenate([segment, lax.ppermute(segment, "col", pairs)], axis=1)

    smem = pl.BlockSpec(memory_space=pltpu.SMEM)
    vmem = pl.BlockSpec(memory_space=pltpu.VMEM)
    rows_type = jax.ShapeDtypeStruct((slots, vec_count, width), vectors.dtype)
    near_rows, far_picked = pl.pallas_call(
        functools.partial(pick_kernel, digits=digits, per_piece=per_piece),
        out_shape=(rows_type, rows_type),
        in_specs=[smem, smem, smem, vmem],
        out_specs=(vmem, vmem),
    )(pair_cols, far_index, own, segment)
    far_rows = lax.ppermute(far_picked, both, down)
    live = (jnp.arange(slots) < count)[:, None, None]
    normal = jnp.einsum("kva,kba->kvb", near_rows, blocks, preferred_element_type=jnp.float32)
    normal = jnp.where(live, normal, 0.0)
    arrived = lax.ppermute(normal, both, up)
    trans = jnp.einsum("kvb,kba->kva", far_rows, blocks, preferred_element_type=jnp.float32)

    total = pl.pallas_call(
        functools.partial(add_kernel, digits=digits, per_piece=per_piece),
        out_shape=jax.ShapeDtypeStruct((vec_count, piece * col_count), jnp.float32),
        in_specs=[smem, smem, smem, smem, vmem, vmem],
        out_specs=vmem,
    )(pair_cols, far_index, own, count[None], trans, arrived)
    for bit in range(digits):
        pairs = [(c, c ^ (1 << bit)) for c in range(col_count)]
        half = total.shape[1] // 2
        total = total[:, :half] + lax.ppermute(total[:, half:], "col", pairs)
    return total


def solution(mesh):
    in_specs = (
        P(None, ("row", "col")),
        P("row", "col", None, None, None),
        P("row", "col", None, None),
        P("row", "col"),
    )
    out_specs = P(None, ("row", "col"))
    return jax.shard_map(body, mesh=mesh, in_specs=in_specs, out_specs=out_specs, check_vma=False)
```

```python
import jax
import jax.numpy as jnp
from jax import lax
from jax.experimental import pallas as pl
from jax.experimental.pallas import tpu as pltpu
from jax.sharding import PartitionSpec as P

SERVER = (
    (4, 5, 3, 2, 9, 0, 1, 14, 15, 12, 11, 10, 13, 8, 6, 7),
    (7, 1, 2, 4, 5, 6, 0, 3, 15, 14, 11, 13, 8, 10, 9, 12),
    (5, 2, 9, 6, 4, 7, 1, 15, 14, 0, 3, 8, 10, 12, 13, 11),
    (2, 0, 6, 4, 7, 8, 5, 9, 12, 14, 1, 3, 15, 11, 10, 13),
)
SMEM = pl.BlockSpec(memory_space=pltpu.SMEM)
VMEM = pl.BlockSpec(memory_space=pltpu.VMEM)


def block_slice(block, width, per_piece):
    return pl.ds(pl.multiple_of(block % per_piece * width, width), width)


def pick_kernel(index, segment, rows):
    slots, _, width = rows.shape
    per_piece = segment.shape[-1] // width
    for slot in range(slots):
        block = index[slot]
        rows[slot] = segment[block // per_piece, :, block_slice(block, width, per_piece)]


def place_first_kernel(index, own_ref, rows, total):
    slots, _, width = rows.shape
    per_piece = total.shape[-1] // width
    own = own_ref[0]
    total[...] = jnp.zeros_like(total)
    for slot in range(slots):
        block = index[slot]
        piece = block // per_piece
        total[(piece ^ own) & 1, piece // 2, :, block_slice(block, width, per_piece)] += rows[slot]


def place_second_kernel(index, own_ref, count_ref, rows, earlier, keep, send, total):
    slots, _, width = rows.shape
    per_piece = total.shape[-1] // width
    own = own_ref[0]
    count = count_ref[0]
    total[...] = earlier[...]
    for slot in range(slots):
        block = index[slot]
        piece = block // per_piece
        value = jnp.where(slot < count, rows[slot], 0.0)
        total[(piece ^ own) & 1, piece // 2, :, block_slice(block, width, per_piece)] += value
    send[...] = total[1]
    keep[...] = total[0]


def body(vectors, tile_blocks, block_pairs, tile_counts):
    row_count = lax.axis_size("row")
    col_count = lax.axis_size("col")
    col_index = lax.axis_index("col")
    row_index = lax.axis_index("row")
    blocks = tile_blocks[0, 0]
    pair_rows = block_pairs[0, 0, :, 0]
    pair_cols = block_pairs[0, 0, :, 1]
    slots, width, _ = blocks.shape
    vec_count, piece = vectors.shape
    half_count = col_count // 2
    own = col_index.astype(jnp.int32)[None]
    in_band = row_index + col_index < row_count
    count = jnp.where(in_band, tile_counts[0, 0], 0)
    live = (jnp.arange(slots) < count)[:, None, None]
    both = ("row", "col")
    up = [(r * col_count + c, (r + c) * col_count + SERVER[(r + c) % 4][c])
          for r in range(row_count) for c in range(col_count) if r + c < row_count]
    down = [(b, a) for a, b in up]

    far_index = lax.ppermute(jnp.broadcast_to(pair_rows, (16, slots)), both, up)[0]
    copies = jnp.broadcast_to(vectors, (col_count, vec_count, piece))
    segment = lax.all_to_all(copies, "col", 0, 0, tiled=True)

    cost = pl.CostEstimate(flops=0, bytes_accessed=1000000, transcendentals=0)
    rows_type = jax.ShapeDtypeStruct((slots, vec_count, width), vectors.dtype)
    pick = pl.pallas_call(
        pick_kernel, out_shape=rows_type, in_specs=[SMEM, VMEM], out_specs=VMEM, cost_estimate=cost,
    )
    normal = jnp.einsum("kva,kba->kvb", pick(pair_cols, segment), blocks, preferred_element_type=jnp.float32)
    normal = jnp.where(live, normal, 0.0)
    arrived = lax.ppermute(normal, both, up)
    late_index, _ = lax.optimization_barrier((far_index, normal))
    far_rows = lax.ppermute(pick(late_index, segment), both, down)

    halves = (2, half_count, vec_count, piece)
    normal_total = pl.pallas_call(
        place_first_kernel,
        out_shape=jax.ShapeDtypeStruct(halves, jnp.float32),
        in_specs=[SMEM, SMEM, VMEM], out_specs=VMEM, cost_estimate=cost,
    )(far_index, own, arrived)
    far_rows, normal_total = lax.optimization_barrier((far_rows, normal_total))
    trans = jnp.einsum("kvb,kba->kva", far_rows, blocks, preferred_element_type=jnp.float32)
    half_type = jax.ShapeDtypeStruct(halves[1:], jnp.float32)
    keep, send = pl.pallas_call(
        place_second_kernel,
        out_shape=(half_type, half_type),
        in_specs=[SMEM, SMEM, SMEM, VMEM, VMEM], out_specs=(VMEM, VMEM),
        scratch_shapes=[pltpu.VMEM(halves, jnp.float32)], cost_estimate=cost,
    )(pair_cols, own, count[None], trans, normal_total)

    swap = [(c, c ^ 1) for c in range(col_count)]
    groups = [list(range(core, col_count, 2)) for core in range(2)]
    total = keep + lax.ppermute(send, "col", swap)
    parts = lax.all_to_all(total, "col", 0, 0, axis_index_groups=groups, tiled=True)
    return jnp.sum(parts, axis=0)


def solution(mesh):
    in_specs = (
        P(None, ("row", "col")),
        P("row", "col", None, None, None),
        P("row", "col", None, None),
        P("row", "col"),
    )
    out_specs = P(None, ("row", "col"))
    return jax.shard_map(body, mesh=mesh, in_specs=in_specs, out_specs=out_specs, check_vma=False)
```

```python
import jax
import jax.numpy as jnp
from jax import lax
from jax.experimental import pallas as pl
from jax.experimental.pallas import tpu as pltpu
from jax.sharding import PartitionSpec as P

SERVER = (
    (4, 5, 3, 2, 9, 0, 1, 14, 15, 12, 11, 10, 13, 8, 6, 7),
    (7, 1, 2, 4, 5, 6, 0, 3, 15, 14, 11, 13, 8, 10, 9, 12),
    (5, 2, 9, 6, 4, 7, 1, 15, 14, 0, 3, 8, 10, 12, 13, 11),
    (2, 0, 6, 4, 7, 8, 5, 9, 12, 14, 1, 3, 15, 11, 10, 13),
)
SMEM = pl.BlockSpec(memory_space=pltpu.SMEM)
VMEM = pl.BlockSpec(memory_space=pltpu.VMEM)


def in_vmem(array):
    return pltpu.with_memory_space_constraint(array, pltpu.VMEM)


def block_slice(block, width, per_piece):
    return pl.ds(pl.multiple_of(block % per_piece * width, width), width)


def pick_kernel(index, segment, rows):
    slots, _, width = rows.shape
    per_piece = segment.shape[-1] // width
    for slot in range(slots):
        block = index[slot]
        rows[slot] = segment[block // per_piece, :, block_slice(block, width, per_piece)]


def place_kernel(index, far_index, own_ref, count_ref, trans, arrived, late, keep, send, total):
    slots, _, width = trans.shape
    per_piece = total.shape[-1] // width
    own = own_ref[0]
    count = count_ref[0]
    total[...] = jnp.zeros_like(total)
    for slot in range(slots):
        product = jnp.where(slot < count, trans[slot], 0.0)
        for block, value in ((index[slot], product), (far_index[slot], arrived[slot] + late[slot])):
            piece = block // per_piece
            total[(piece ^ own) & 1, piece // 2, :, block_slice(block, width, per_piece)] += value
    send[...] = total[1]
    keep[...] = total[0]


def body(vectors, tile_blocks, block_pairs, tile_counts):
    row_count = lax.axis_size("row")
    col_count = lax.axis_size("col")
    col_index = lax.axis_index("col")
    row_index = lax.axis_index("row")
    blocks = tile_blocks[0, 0]
    pair_rows = block_pairs[0, 0, :, 0]
    pair_cols = block_pairs[0, 0, :, 1]
    slots, width, _ = blocks.shape
    vec_count, piece = vectors.shape
    half_count = col_count // 2
    own = col_index.astype(jnp.int32)[None]
    in_band = row_index + col_index < row_count
    count = jnp.where(in_band, tile_counts[0, 0], 0)
    live = (jnp.arange(slots) < count)[:, None, None]
    both = ("row", "col")
    up = [(r * col_count + c, (r + c) * col_count + SERVER[(r + c) % 4][c])
          for r in range(row_count) for c in range(col_count) if r + c < row_count]
    down = [(b, a) for a, b in up]

    def slack(tile, server):
        part = [device // col_count // 4 % 4 for device in (tile, server)]
        return part[1] == 2 or (part[0] == 0 and part[1] == 3)

    far_index = lax.ppermute(jnp.broadcast_to(pair_rows, (16, slots)), both, up)[0]
    copies = jnp.broadcast_to(vectors, (col_count, vec_count, piece))
    segment = lax.all_to_all(copies, "col", 0, 0, tiled=True)

    cost = pl.CostEstimate(flops=0, bytes_accessed=1000000, transcendentals=0)
    call = pl.pallas_call(
        pick_kernel, out_shape=pltpu.VMEM((slots, vec_count, width), vectors.dtype),
        in_specs=[SMEM, VMEM], out_specs=VMEM, cost_estimate=cost,
    )

    def pick(index):
        return call(index, in_vmem(segment))

    normal = jnp.einsum("kva,kba->kvb", pick(pair_cols), blocks, preferred_element_type=jnp.float32)
    normal = jnp.where(live, normal, 0.0)
    arrived = lax.ppermute(normal, both, [(a, b) for a, b in up if not slack(a, b)])
    late_index, _ = lax.optimization_barrier((far_index, normal))
    far_picked = pick(late_index)
    far_rows = lax.ppermute(far_picked, both, down)
    late_normal, _ = lax.optimization_barrier((normal, far_picked))
    late = lax.ppermute(late_normal, both, [(a, b) for a, b in up if slack(a, b)])

    halves = (2, half_count, vec_count, piece)
    far_rows, arrived = lax.optimization_barrier((far_rows, arrived))
    trans = jnp.einsum("kvb,kba->kva", far_rows, blocks, preferred_element_type=jnp.float32)
    half_type = pltpu.VMEM(halves[1:], jnp.float32)
    keep, send = pl.pallas_call(
        place_kernel,
        out_shape=(half_type, half_type),
        in_specs=[SMEM] * 4 + [VMEM] * 3, out_specs=(VMEM, VMEM),
        scratch_shapes=[pltpu.VMEM(halves, jnp.float32)], cost_estimate=cost,
    )(pair_cols, far_index, own, count[None], in_vmem(trans), in_vmem(arrived), in_vmem(late))

    swap = [(c, c ^ 1) for c in range(col_count)]
    groups = [list(range(core, col_count, 2)) for core in range(2)]
    total = keep + lax.ppermute(send, "col", swap)
    parts = lax.all_to_all(total, "col", 0, 0, axis_index_groups=groups, tiled=True)
    return jnp.sum(parts, axis=0)


def solution(mesh):
    in_specs = (
        P(None, ("row", "col")),
        P("row", "col", None, None, None),
        P("row", "col", None, None),
        P("row", "col"),
    )
    out_specs = P(None, ("row", "col"))
    return jax.shard_map(body, mesh=mesh, in_specs=in_specs, out_specs=out_specs, check_vma=False)
```

```python
import jax
import jax.numpy as jnp
from jax import lax
from jax.experimental import pallas as pl
from jax.experimental.pallas import tpu as pltpu
from jax.sharding import PartitionSpec as P

SERVER = (
    (6, 5, 4, 7, 2, 14, 0, 1, 3, 12, 15, 10, 13, 11, 9, 8),
    (2, 7, 3, 5, 4, 6, 1, 14, 15, 0, 13, 11, 12, 9, 8, 10),
    (6, 3, 4, 5, 2, 7, 8, 15, 0, 14, 1, 11, 9, 10, 13, 12),
    (8, 3, 7, 6, 9, 4, 5, 11, 0, 14, 1, 2, 10, 12, 13, 15),
)
SMEM = pl.BlockSpec(memory_space=pltpu.SMEM)
VMEM = pl.BlockSpec(memory_space=pltpu.VMEM)


def in_vmem(array):
    return pltpu.with_memory_space_constraint(array, pltpu.VMEM)


def block_slice(block, width, per_piece):
    return pl.ds(pl.multiple_of(block % per_piece * width, width), width)


def pick_kernel(index, segment, rows):
    slots, _, width = rows.shape
    per_piece = segment.shape[-1] // width
    for slot in range(slots):
        block = index[slot]
        rows[slot] = segment[block // per_piece, :, block_slice(block, width, per_piece)]


def place_kernel(index, far_index, own_ref, count_ref, trans, arrived, late, keep, send, total):
    slots, _, width = trans.shape
    per_piece = total.shape[-1] // width
    own = own_ref[0]
    count = count_ref[0]
    total[...] = jnp.zeros_like(total)
    for slot in range(slots):
        product = jnp.where(slot < count, trans[slot], 0.0)
        for block, value in ((index[slot], product), (far_index[slot], arrived[slot] + late[slot])):
            piece = block // per_piece
            total[(piece ^ own) & 1, piece // 2, :, block_slice(block, width, per_piece)] += value
    send[...] = total[1]
    keep[...] = total[0]


def body(vectors, tile_blocks, block_pairs, tile_counts):
    row_count = lax.axis_size("row")
    col_count = lax.axis_size("col")
    col_index = lax.axis_index("col")
    row_index = lax.axis_index("row")
    blocks = tile_blocks[0, 0]
    pair_rows = block_pairs[0, 0, :, 0]
    pair_cols = block_pairs[0, 0, :, 1]
    slots, width, _ = blocks.shape
    vec_count, piece = vectors.shape
    half_count = col_count // 2
    own = col_index.astype(jnp.int32)[None]
    in_band = row_index + col_index < row_count
    count = jnp.where(in_band, tile_counts[0, 0], 0)
    live = (jnp.arange(slots) < count)[:, None, None]
    both = ("row", "col")
    up = [(r * col_count + c, (r + c) * col_count + SERVER[(r + c) % 4][c])
          for r in range(row_count) for c in range(col_count) if r + c < row_count]
    down = [(b, a) for a, b in up]

    def slack(tile, server):
        part = [device // col_count // 4 % 4 for device in (tile, server)]
        return part[1] == 2 or (part[0] == 0 and part[1] == 3)

    far_index = lax.ppermute(jnp.broadcast_to(pair_rows, (16, slots)), both, up)[0]
    copies = jnp.broadcast_to(vectors, (col_count, vec_count, piece))
    segment = lax.all_to_all(copies, "col", 0, 0, tiled=True)

    cost = pl.CostEstimate(flops=0, bytes_accessed=1000000, transcendentals=0)
    call = pl.pallas_call(
        pick_kernel, out_shape=pltpu.VMEM((slots, vec_count, width), vectors.dtype),
        in_specs=[SMEM, VMEM], out_specs=VMEM, cost_estimate=cost,
    )

    def pick(index):
        return call(index, in_vmem(segment))

    normal = jnp.einsum("kva,kba->kvb", pick(pair_cols), blocks, preferred_element_type=jnp.float32)
    normal = jnp.where(live, normal, 0.0)
    arrived = lax.ppermute(normal, both, [(a, b) for a, b in up if not slack(a, b)])
    late_index, _ = lax.optimization_barrier((far_index, normal))
    far_picked = pick(late_index)
    far_rows = lax.ppermute(far_picked, both, down)
    late_normal, _ = lax.optimization_barrier((normal, far_picked))
    late = lax.ppermute(late_normal, both, [(a, b) for a, b in up if slack(a, b)])

    halves = (2, half_count, vec_count, piece)
    far_rows, arrived = lax.optimization_barrier((far_rows, arrived))
    trans = jnp.einsum("kvb,kba->kva", far_rows, blocks, preferred_element_type=jnp.float32)
    half_type = pltpu.VMEM(halves[1:], jnp.float32)
    keep, send = pl.pallas_call(
        place_kernel,
        out_shape=(half_type, half_type),
        in_specs=[SMEM] * 4 + [VMEM] * 3, out_specs=(VMEM, VMEM),
        scratch_shapes=[pltpu.VMEM(halves, jnp.float32)], cost_estimate=cost,
    )(pair_cols, far_index, own, count[None], in_vmem(trans), in_vmem(arrived), in_vmem(late))

    swap = [(c, c ^ 1) for c in range(col_count)]
    groups = [list(range(core, col_count, 2)) for core in range(2)]
    total = keep + lax.ppermute(send, "col", swap)
    parts = lax.all_to_all(total, "col", 0, 0, axis_index_groups=groups, tiled=True)
    return jnp.sum(parts, axis=0)


def solution(mesh):
    in_specs = (
        P(None, ("row", "col")),
        P("row", "col", None, None, None),
        P("row", "col", None, None),
        P("row", "col"),
    )
    out_specs = P(None, ("row", "col"))
    return jax.shard_map(body, mesh=mesh, in_specs=in_specs, out_specs=out_specs, check_vma=False)
```

```python
import jax
import jax.numpy as jnp
from jax import lax
from jax.experimental import pallas as pl
from jax.experimental.pallas import tpu as pltpu
from jax.sharding import PartitionSpec as P

SERVER = (
    (6, 5, 4, 7, 2, 14, 0, 1, 3, 12, 15, 10, 13, 11, 9, 8),
    (2, 7, 3, 5, 4, 6, 1, 14, 15, 0, 13, 11, 12, 9, 8, 10),
    (6, 3, 4, 5, 2, 7, 8, 15, 0, 14, 1, 11, 9, 10, 13, 12),
    (8, 3, 7, 6, 9, 4, 5, 11, 0, 14, 1, 2, 10, 12, 13, 15),
)
SMEM = pl.BlockSpec(memory_space=pltpu.SMEM)
VMEM = pl.BlockSpec(memory_space=pltpu.VMEM)


def in_vmem(array):
    return pltpu.with_memory_space_constraint(array, pltpu.VMEM)


def block_slice(block, width, per_piece):
    return pl.ds(pl.multiple_of(block % per_piece * width, width), width)


def pick_kernel(index, segment, rows):
    slots, _, width = rows.shape
    per_piece = segment.shape[-1] // width
    for slot in range(slots):
        block = index[slot]
        rows[slot] = segment[block // per_piece, :, block_slice(block, width, per_piece)]


def place_kernel(index, far_index, own_ref, count_ref, trans, arrived, late, keep, send, total):
    slots, _, width = trans.shape
    per_piece = total.shape[-1] // width
    own = own_ref[0]
    count = count_ref[0]
    total[...] = jnp.zeros_like(total)
    for slot in range(slots):
        product = jnp.where(slot < count, trans[slot], 0.0)
        for block, value in ((index[slot], product), (far_index[slot], arrived[slot] + late[slot])):
            piece = block // per_piece
            total[(piece ^ own) & 1, piece // 2, :, block_slice(block, width, per_piece)] += value
    send[...] = total[1]
    keep[...] = total[0]


def body(vectors, tile_blocks, block_pairs, tile_counts):
    row_count = lax.axis_size("row")
    col_count = lax.axis_size("col")
    col_index = lax.axis_index("col")
    row_index = lax.axis_index("row")
    blocks = tile_blocks[0, 0]
    pair_rows = block_pairs[0, 0, :, 0]
    pair_cols = block_pairs[0, 0, :, 1]
    slots, width, _ = blocks.shape
    vec_count, piece = vectors.shape
    half_count = col_count // 2
    own = col_index.astype(jnp.int32)[None]
    in_band = row_index + col_index < row_count
    count = jnp.where(in_band, tile_counts[0, 0], 0)
    live = (jnp.arange(slots) < count)[:, None, None]
    both = ("row", "col")
    up = [(r * col_count + c, (r + c) * col_count + SERVER[(r + c) % 4][c])
          for r in range(row_count) for c in range(col_count) if r + c < row_count]
    down = [(b, a) for a, b in up]

    def slack(tile, server):
        part = [device // col_count // 4 % 4 for device in (tile, server)]
        return part[0] == 0 and part[1] >= 2

    far_index = lax.ppermute(jnp.broadcast_to(pair_rows, (16, slots)), both, up)[0]
    copies = jnp.broadcast_to(vectors, (col_count, vec_count, piece))
    segment = lax.all_to_all(copies, "col", 0, 0, tiled=True)

    cost = pl.CostEstimate(flops=0, bytes_accessed=1000000, transcendentals=0)
    call = pl.pallas_call(
        pick_kernel, out_shape=pltpu.VMEM((slots, vec_count, width), vectors.dtype),
        in_specs=[SMEM, VMEM], out_specs=VMEM, cost_estimate=cost,
    )

    def pick(index):
        return call(index, in_vmem(segment))

    normal = jnp.einsum("kva,kba->kvb", pick(pair_cols), blocks, preferred_element_type=jnp.float32)
    normal = jnp.where(live, normal, 0.0)
    arrived = lax.ppermute(normal, both, [(a, b) for a, b in up if not slack(a, b)])
    late_index, _ = lax.optimization_barrier((far_index, normal))
    far_picked = pick(late_index)
    far_rows = lax.ppermute(far_picked, both, down)
    late_normal, _ = lax.optimization_barrier((normal, far_picked))
    late = lax.ppermute(late_normal, both, [(a, b) for a, b in up if slack(a, b)])

    halves = (2, half_count, vec_count, piece)
    far_rows, arrived = lax.optimization_barrier((far_rows, arrived))
    trans = jnp.einsum("kvb,kba->kva", far_rows, blocks, preferred_element_type=jnp.float32)
    half_type = pltpu.VMEM(halves[1:], jnp.float32)
    keep, send = pl.pallas_call(
        place_kernel,
        out_shape=(half_type, half_type),
        in_specs=[SMEM] * 4 + [VMEM] * 3, out_specs=(VMEM, VMEM),
        scratch_shapes=[pltpu.VMEM(halves, jnp.float32)], cost_estimate=cost,
    )(pair_cols, far_index, own, count[None], in_vmem(trans), in_vmem(arrived), in_vmem(late))

    swap = [(c, c ^ 1) for c in range(col_count)]
    groups = [list(range(core, col_count, 2)) for core in range(2)]
    total = keep + lax.ppermute(send, "col", swap)
    parts = lax.all_to_all(total, "col", 0, 0, axis_index_groups=groups, tiled=True)
    return jnp.sum(parts, axis=0)


def solution(mesh):
    in_specs = (
        P(None, ("row", "col")),
        P("row", "col", None, None, None),
        P("row", "col", None, None),
        P("row", "col"),
    )
    out_specs = P(None, ("row", "col"))
    return jax.shard_map(body, mesh=mesh, in_specs=in_specs, out_specs=out_specs, check_vma=False)
```
